1024 devices in a mesh: seg: 64 (over x, y), sub: 16 (over z, core).
Axes of the slice: x: 8, y: 8, z: 8, core: 2. Of those that a mesh axis runs over, the one named last changes fastest.
Arguments:
- multipoles: float32 [121, 524288], P(None, ('seg', 'sub')), may hold values from -6 to 6
- top_multipoles: float32 [121, 1024], P(None, ('seg', 'sub')), may hold values from -6 to 6
- translators: float32 [16, 121, 121], replicated, may hold values from -0.5 to 0.5
- child_shifts: float32 [8, 121, 121], replicated, may hold values from -0.5 to 0.5
- far_operator: float32 [121, 121], replicated, may hold values from -0.5 to 0.5
- far_weights: float32 [65536, 1024], P(('seg', 'sub')), may hold values from -0.1875 to 0.1875
- cell_codes: int32 [1024, 512], P(('seg', 'sub')), may hold values from 0 to 511, each once within a row
- inner_sources: int32 [1024, 16, 64], P(('seg', 'sub')), may hold values from 0 to 543
- inner_targets: int32 [1024, 16, 64], P(('seg', 'sub')), may hold values from 0 to 511
- pair_sources: int32 [1024, 16, 16, 8], P(('seg', 'sub')), may hold values from 0 to 511
- peer_target_cells: int32 [1024, 16, 16, 8], P(('seg', 'sub')), may hold values from 0 to 511
- pair_counts: int32 [1024, 16, 16], P(('seg', 'sub')), may hold values from 0 to 8, as said below
Outputs:
- local_field: float32 [121, 524288], P(None, ('seg', 'sub'))
The draws below stay inside these ranges and needn't reach their ends.
Inputs may be any that keep to these rules, and one draw needn't show every extreme that they name: `pair_counts`: for each device and peer the counts over all relative positions sum to at most 64; every device has a peer whose counts sum to exactly 64, each of them 0 or 8; which peer and positions is drawn. `cell_codes`: each device's codes are a permutation of 0 to 511.
All inputs are finite; a program needn't handle non-finite values.
Results may differ from the reference program's by a relative error of at most 0.0003.
Values sent between devices are 32-bit elements; how exact they have to be, the bound alone decides.
No kernel may reach another device: no remote copies, remote signals or barrier semaphores. Data moves between devices by JAX's collectives and lax.ppermute only.
A program may use at most 32 MiB of HBM per device.

```python
import jax
import jax.numpy as jnp
from jax import lax

ORDER = 10
COEF = 121
CELL_DEV = 512
PAR_DEV = 64
NOFF = 16
CAP = 8
PACK = 64
INNER_CAP = 64
HALO = 16
CELLS = 524288
PARENTS = 65536
TOPCELLS = 1024
N_SUB = 16
DEVICES = 1024


def draw_pair_counts(key, part):
    key = jax.random.fold_in(key, 5)
    first, second, third, fourth = jax.random.split(key, 4)
    level = jax.random.randint(first, (DEVICES, 1, 1), 1, 5)
    raw = jax.random.randint(second, (DEVICES, N_SUB, NOFF), 0, CAP + 1)
    counts = raw * level // 4
    total = jnp.sum(counts, axis=2, keepdims=True)
    counts = counts * PACK // jnp.maximum(total, PACK)
    busy = jax.random.randint(third, (DEVICES, 1, 1), 0, N_SUB)
    scores = jax.random.randint(fourth, (DEVICES, 1, NOFF), 0, 1 << 20) * NOFF + jnp.arange(NOFF)[None, None, :]
    rank = jnp.argsort(jnp.argsort(scores, axis=2), axis=2)
    full = jnp.where(rank < PACK // CAP, CAP, 0)
    spot = jnp.arange(N_SUB)[None, :, None] == busy
    return jnp.where(spot, full, counts).astype(jnp.int32)


def plant(drawn, stream_key, least, high):
    extent = drawn.shape
    place = [jax.random.randint(jax.random.fold_in(stream_key, axis), (), 0, extent[axis]) for axis in range(len(extent))]
    drawn = drawn.at[tuple(place)].set(least)
    longest = extent.index(max(extent))
    place[longest] = (place[longest] + 1) % extent[longest]
    return drawn.at[tuple(place)].set(high)


def levels(key, shape, cuts, least, top_value):
    level, own = 1.0, jax.random.fold_in(key, 6)
    for axis_at, blocks in cuts:
        heights = jnp.exp(jax.random.uniform(jax.random.fold_in(own, axis_at), (blocks,), jnp.float32, least / len(cuts), top_value / len(cuts)))
        level = level * jnp.repeat(heights, shape[axis_at] // blocks).reshape([-1 if axis == axis_at else 1 for axis in range(len(shape))])
    return level


def normal_values(own_key, extent, deviation, reach, shards=(), held_as=jnp.bfloat16):
    loudness = levels(own_key, extent, shards, -0.22, 0.18) if shards else 1.0
    values = jax.random.normal(own_key, extent, jnp.float32) * deviation * loudness
    return jnp.minimum(jnp.maximum(values, -reach), reach).astype(held_as)


def setup_inputs(seed: int = 0) -> dict:
    keys = jax.random.split(jax.random.key(seed), 13)
    multipoles = normal_values(keys[0], (COEF, CELLS), 1.0, 6.0, ((1, 1024),), jnp.float32)
    top_multipoles = normal_values(keys[1], (COEF, TOPCELLS), 1.0, 6.0, ((1, 1024),), jnp.float32)
    translators = normal_values(keys[2], (NOFF, COEF, COEF), COEF ** -0.5, 0.5, (), jnp.float32)
    child_shifts = normal_values(keys[3], (8, COEF, COEF), COEF ** -0.5, 0.5, (), jnp.float32)
    far_operator = normal_values(keys[4], (COEF, COEF), COEF ** -0.5, 0.5, (), jnp.float32)
    far_weights = normal_values(keys[5], (PARENTS, TOPCELLS), TOPCELLS ** -0.5, 0.1875, ((0, 1024),), jnp.float32)
    cell_codes = jax.vmap(lambda own: jax.random.permutation(own, CELL_DEV))(jax.random.split(keys[6], DEVICES)).reshape((DEVICES, CELL_DEV)).astype(jnp.int32)
    inner_sources = plant(jax.random.randint(keys[7], (DEVICES, NOFF, INNER_CAP), 0, CELL_DEV + 2 * HALO), jax.random.fold_in(keys[7], 1), 0, (CELL_DEV + 2 * HALO) - 1).astype(jnp.int32)
    inner_targets = plant(jax.random.randint(keys[8], (DEVICES, NOFF, INNER_CAP), 0, CELL_DEV), jax.random.fold_in(keys[8], 1), 0, CELL_DEV - 1).astype(jnp.int32)
    pair_sources = plant(jax.random.randint(keys[9], (DEVICES, N_SUB, NOFF, CAP), 0, CELL_DEV), jax.random.fold_in(keys[9], 1), 0, CELL_DEV - 1).astype(jnp.int32)
    peer_target_cells = plant(jax.random.randint(keys[10], (DEVICES, N_SUB, NOFF, CAP), 0, CELL_DEV), jax.random.fold_in(keys[10], 1), 0, CELL_DEV - 1).astype(jnp.int32)
    pair_counts = draw_pair_counts(jax.random.fold_in(keys[12], 71), 0)
    return dict(multipoles=multipoles, top_multipoles=top_multipoles, translators=translators, child_shifts=child_shifts, far_operator=far_operator, far_weights=far_weights, cell_codes=cell_codes, inner_sources=inner_sources, inner_targets=inner_targets, pair_sources=pair_sources, peer_target_cells=peer_target_cells, pair_counts=pair_counts)


UPPER_LEVEL = lax.Precision.HIGHEST


def degree_signs():
    index = jnp.arange(COEF)
    degree = jnp.zeros((COEF,), jnp.int32)
    for level in range(1, ORDER + 1):
        degree = degree + (index >= level * level).astype(jnp.int32)
    return (1 - 2 * (degree % 2)).astype(jnp.float32)


def reference(multipoles, top_multipoles, translators, child_shifts, far_operator, far_weights, cell_codes, inner_sources, inner_targets, pair_sources, peer_target_cells, pair_counts):
    signs = degree_signs()
    sign_adjusted = translators * signs[None, :, None] * signs[None, None, :]
    groups = DEVICES // N_SUB
    summed = jnp.dot(top_multipoles, far_weights.T, precision=UPPER_LEVEL)
    parent_local = jnp.dot(far_operator, summed, precision=UPPER_LEVEL)
    parent_dev = parent_local.reshape(COEF, DEVICES, PAR_DEV).transpose(1, 0, 2)
    per_dev = multipoles.reshape(COEF, DEVICES, CELL_DEV).transpose(1, 0, 2)
    grid = per_dev.reshape(groups, N_SUB, COEF, CELL_DEV)
    blank = jnp.zeros((1, N_SUB, COEF, HALO), jnp.float32)
    before = jnp.concatenate([blank, grid[:-1, :, :, CELL_DEV - HALO:]], axis=0)
    after = jnp.concatenate([grid[1:, :, :, :HALO], blank], axis=0)
    window = jnp.concatenate([before, grid, after], axis=3).reshape(DEVICES, COEF, CELL_DEV + 2 * HALO)
    codes = cell_codes.reshape(DEVICES, CELL_DEV)

    def one_device(items):
        parent, code, ext, isrc, idst = items
        at_cell = parent[:, code // 8]
        shifted = jnp.einsum('okj,jn->okn', child_shifts, at_cell, precision=UPPER_LEVEL)
        pick = (code[None, :] % 8 == jnp.arange(8)[:, None]).astype(jnp.float32)
        field = jnp.sum(shifted * pick[:, None, :], axis=0)
        src = ext[:, isrc]
        contrib = jnp.einsum('okj,joc->koc', translators, src, precision=UPPER_LEVEL)
        return field.at[:, idst.reshape(-1)].add(contrib.reshape(COEF, -1))

    near = lax.map(one_device, (parent_dev, codes, window, inner_sources, inner_targets))

    src_all = pair_sources.reshape(groups, N_SUB, N_SUB, NOFF, CAP)
    dst_all = peer_target_cells.reshape(groups, N_SUB, N_SUB, NOFF, CAP)
    cnt_all = pair_counts.reshape(groups, N_SUB, N_SUB, NOFF)

    def one_group(items):
        cells, src, dst, cnt = items
        flat = cells.transpose(1, 0, 2).reshape(COEF, N_SUB * CELL_DEV)
        valid_mask = (jnp.arange(CAP)[None, None, None, :] < cnt[..., None]).astype(jnp.float32)
        owner = jnp.arange(N_SUB)[:, None, None, None] * CELL_DEV
        peer = jnp.arange(N_SUB)[None, :, None, None] * CELL_DEV
        src_idx = (src + owner).astype(jnp.int32)
        dst_idx = (dst + peer).astype(jnp.int32)
        msrc = flat[:, src_idx] * valid_mask[None]
        mdst = flat[:, dst_idx]
        forward = jnp.einsum('okj,jpqoc->kpqoc', translators, msrc, precision=UPPER_LEVEL)
        back = jnp.einsum('okj,jpqoc->kpqoc', sign_adjusted, mdst, precision=UPPER_LEVEL) * valid_mask[None]
        out = jnp.zeros((COEF, N_SUB * CELL_DEV), jnp.float32)
        out = out.at[:, dst_idx.reshape(-1)].add(forward.reshape(COEF, -1))
        out = out.at[:, src_idx.reshape(-1)].add(back.reshape(COEF, -1))
        return out

    pairs = lax.map(one_group, (grid, src_all, dst_all, cnt_all))
    pairs = pairs.reshape(groups, COEF, N_SUB, CELL_DEV).transpose(0, 2, 1, 3).reshape(DEVICES, COEF, CELL_DEV)
    total = near + pairs
    return total.transpose(1, 0, 2).reshape(COEF, CELLS)
```

```python
import jax
import jax.numpy as jnp
from jax import lax
from jax.experimental import pallas as pl
from jax.experimental.pallas import tpu as pltpu
from jax.sharding import PartitionSpec as P

ORDER = 10
HALO = 16
WIDE = 128
F32 = jnp.float32
BF16 = jnp.bfloat16
NT = (((1,), (1,)), ((), ()))
NN = (((1,), (0,)), ((), ()))


def degree_signs(coefs):
    index = lax.broadcasted_iota(jnp.int32, (1, coefs), 1)
    degree = jnp.zeros((1, coefs), jnp.int32)
    for level in range(1, ORDER + 1):
        degree = degree + (index >= level * level).astype(jnp.int32)
    return (1 - 2 * (degree % 2)).astype(F32)


def two_terms(value):
    high = value.astype(BF16)
    return high, (value - high.astype(F32)).astype(BF16)


def both_terms(value, axis):
    return jnp.concatenate(two_terms(value), axis=axis)


def dot(left, right, dims):
    return lax.dot_general(left, right, dims, preferred_element_type=F32)


def dot_exact(left, right, dims):
    return lax.dot_general(
        left, right, dims, precision=lax.Precision.HIGHEST, preferred_element_type=F32
    )


def halves(value):
    return value[:, :WIDE] + value[:, WIDE:]


def as_columns(row):
    return jnp.transpose(jnp.broadcast_to(row, (WIDE, row.shape[1])))


def source_indicator(row, cells):
    columns = as_columns(row)
    parts = []
    for at in range(0, cells, WIDE):
        lane = lax.broadcasted_iota(jnp.int32, columns.shape, 1).astype(F32) + float(at)
        parts.append(jnp.where(columns == lane, 1.0, 0.0).astype(BF16))
    return jnp.concatenate(parts, axis=1)


def target_indicator(row, cells):
    shape = (cells, row.shape[1])
    cell = lax.broadcasted_iota(jnp.int32, shape, 0).astype(F32)
    return jnp.where(jnp.broadcast_to(row, shape) == cell, 1.0, 0.0).astype(BF16)


def translate(columns, operator):
    high, low = two_terms(columns)
    op_high, op_low = two_terms(operator)
    return (
        dot(high, op_high, NT) + dot(low, op_high, NT) + dot(high, op_low, NT)
    )


def inner_kernel(window_ref, source_ref, target_ref, operator_ref, out_ref, moved, total):
    offsets = operator_ref.shape[0]
    cells = out_ref.shape[0]
    span = window_ref.shape[1]
    slots = source_ref.shape[1]
    rows = source_ref.shape[0]
    each = rows * slots // offsets
    window = both_terms(window_ref[...], 0)
    for r in range(rows):
        picked = dot(source_indicator(source_ref[r : r + 1, :], span), window, NT)
        moved[r * slots : (r + 1) * slots, :] = halves(picked)
    total[...] = jnp.zeros_like(total)
    for r in range(rows):
        terms = []
        for o in range(r * slots // each, (r + 1) * slots // each):
            terms.append(translate(moved[o * each : (o + 1) * each, :], operator_ref[o]))
        terms = jnp.concatenate(terms, axis=0)
        total[...] += dot(target_indicator(target_ref[r : r + 1, :], cells), both_terms(terms, 1), NN)
    out_ref[...] = halves(total[...])


def far_kernel(top_ref, weight_ref, far_ref, shift_ref, place_ref, near_ref, out_ref):
    top = jnp.concatenate([top_ref[0][:, None], top_ref[1][:, None]], axis=1)
    top = top.reshape(-1, WIDE)
    summed = dot_exact(weight_ref[...], top, NN)
    parent = dot_exact(summed, far_ref[...], NT)
    table = jnp.concatenate(
        [dot_exact(parent, shift_ref[o], NT) for o in range(shift_ref.shape[0])], axis=0
    )
    table = both_terms(table, 1)
    cells = near_ref.shape[0]
    slots = 128
    for at in range(0, cells, slots):
        picked = dot(source_indicator(place_ref[:, at : at + slots], table.shape[0]), table, NN)
        out_ref[at : at + slots, :] = near_ref[at : at + slots, :] + halves(picked)


def pair_kernel(cells_ref, source_ref, target_ref, operator_ref, near_ref, out_ref, block, moved, total):
    peer = pl.program_id(0)
    coefs, cells = out_ref.shape
    offsets = operator_ref.shape[0]
    sign = degree_signs(WIDE)

    @pl.when(peer == 0)
    def _():
        block[...] = jnp.zeros_like(block)

    block[:coefs, :] = cells_ref[0]
    held = both_terms(block[...], 0)
    for way in range(2):
        picked = halves(dot(source_indicator(source_ref[0, way : way + 1, :], cells), held, NT))
        if way == 1:
            picked = picked * sign
        moved[:, way, peer] = picked.reshape(offsets, -1, WIDE)

    @pl.when(peer == pl.num_programs(0) - 1)
    def _():
        total[...] = jnp.zeros_like(total)
        for o in range(offsets):
            terms = translate(moved[o].reshape(-1, WIDE), operator_ref[o])
            count = terms.shape[0] // 2
            terms = jnp.concatenate([terms[:count], terms[count:] * sign], axis=0)
            total[...] += dot(target_indicator(target_ref[o : o + 1, :], cells), both_terms(terms, 1), NN)
        result = near_ref[...] + halves(total[...])
        out_ref[...] = jnp.transpose(result)[:coefs, :]


def whole(shape):
    return pl.BlockSpec(shape, lambda *_: (0,) * len(shape))


def body(
    multipoles,
    top_multipoles,
    translators,
    child_shifts,
    far_operator,
    far_weights,
    cell_codes,
    inner_sources,
    inner_targets,
    pair_sources,
    peer_target_cells,
    pair_counts,
):
    coefs, cells = multipoles.shape
    parents = far_weights.shape[0]
    peers, offsets, room = pair_sources.shape[1:]
    slots = offsets * room
    pad = WIDE - coefs
    segs = lax.axis_size("seg")
    params = pltpu.CompilerParams(vmem_limit_bytes=48 * 1024 * 1024)

    group = lax.all_gather(multipoles, "sub", axis=0, tiled=False)

    used = lax.broadcasted_iota(jnp.int32, (peers, offsets, room), 2) < pair_counts[0][..., None]
    own_source = jnp.where(used, pair_sources[0], -1).reshape(peers, slots).astype(F32)
    own_target = jnp.where(used, peer_target_cells[0], -1).reshape(peers, slots).astype(F32)
    top = jnp.broadcast_to(jnp.pad(top_multipoles[:, 0], (0, pad))[None], (peers, WIDE))
    message = jnp.stack([own_source, own_target, top], axis=1)
    arrived = lax.all_to_all(message, "sub", split_axis=0, concat_axis=0, tiled=True)
    their_source, their_target, tops = arrived[:, 0], arrived[:, 1], arrived[:, 2]

    core = lax.axis_index("sub") % 2
    half = peers // 2
    mine = lax.dynamic_slice_in_dim(tops, core * half, half, axis=0)
    spread = lax.all_to_all(
        jnp.broadcast_to(mine[None], (segs, half, WIDE)), "seg", split_axis=0, concat_axis=0, tiled=True
    )
    every_top = lax.all_gather(
        spread,
        "sub",
        axis=0,
        tiled=False,
        axis_index_groups=[[2 * i, 2 * i + 1] for i in range(half)],
    )

    up = [(i, i + 1) for i in range(segs - 1)]
    down = [(j, i) for i, j in up]
    before = lax.ppermute(multipoles[:, cells - HALO :], "seg", up)
    after = lax.ppermute(multipoles[:, :HALO], "seg", down)
    window = jnp.concatenate([before, multipoles, after], axis=1)
    span = cells + WIDE
    window = jnp.pad(window, ((0, pad), (0, span - window.shape[1])))

    operators = jnp.pad(translators, ((0, 0), (0, pad), (0, pad)))
    shifts = jnp.pad(child_shifts, ((0, 0), (0, pad), (0, pad)))
    far = jnp.pad(far_operator, ((0, pad), (0, pad)))

    inner_rows = inner_sources.shape[1] * inner_sources.shape[2] // 128
    near = pl.pallas_call(
        inner_kernel,
        out_shape=jax.ShapeDtypeStruct((cells, WIDE), F32),
        scratch_shapes=[
            pltpu.VMEM((inner_rows * 128, WIDE), F32),
            pltpu.VMEM((cells, 2 * WIDE), F32),
        ],
        compiler_params=params,
        cost_estimate=pl.CostEstimate(flops=2 * 10**9, bytes_accessed=3 * 10**6, transcendentals=0),
        name="inner_pairs",
    )(
        window,
        inner_sources[0].reshape(inner_rows, 128).astype(F32),
        inner_targets[0].reshape(inner_rows, 128).astype(F32),
        operators,
    )

    octants = child_shifts.shape[0]
    place = (cell_codes % octants * parents + cell_codes // octants).astype(F32)
    near = pl.pallas_call(
        far_kernel,
        out_shape=jax.ShapeDtypeStruct((cells, WIDE), F32),
        compiler_params=params,
        cost_estimate=pl.CostEstimate(flops=10**9, bytes_accessed=2 * 10**6, transcendentals=0),
        name="far_field",
    )(every_top, far_weights, far, shifts, place, near)

    sources = jnp.stack([their_source, own_target], axis=1)
    targets = jnp.stack([their_target, own_source], axis=0)
    targets = targets.reshape(2, peers, offsets, room).transpose(2, 0, 1, 3).reshape(offsets, -1)
    return pl.pallas_call(
        pair_kernel,
        grid=(peers,),
        in_specs=[
            pl.BlockSpec((1, coefs, cells), lambda p: (p, 0, 0)),
            pl.BlockSpec((1, 2, slots), lambda p: (p, 0, 0)),
            whole(targets.shape),
            whole(operators.shape),
            whole(near.shape),
        ],
        out_specs=whole((coefs, cells)),
        out_shape=jax.ShapeDtypeStruct((coefs, cells), F32),
        scratch_shapes=[
            pltpu.VMEM((WIDE, cells), F32),
            pltpu.VMEM((offsets, 2, peers, room, WIDE), F32),
            pltpu.VMEM((cells, 2 * WIDE), F32),
        ],
        compiler_params=params,
        cost_estimate=pl.CostEstimate(flops=6 * 10**9, bytes_accessed=6 * 10**6, transcendentals=0),
        name="pair_terms",
    )(group, sources, targets, operators, near)


def solution(mesh):
    in_specs = (
        P(None, ("seg", "sub")),
        P(None, ("seg", "sub")),
        P(),
        P(),
        P(),
        P(("seg", "sub"), None),
        P(("seg", "sub"), None),
        P(("seg", "sub"), None, None),
        P(("seg", "sub"), None, None),
        P(("seg", "sub"), None, None, None),
        P(("seg", "sub"), None, None, None),
        P(("seg", "sub"), None, None),
    )
    out_specs = P(None, ("seg", "sub"))
    return jax.shard_map(body, mesh=mesh, in_specs=in_specs, out_specs=out_specs, check_vma=False)
```

```python
import jax
import jax.numpy as jnp
from jax import lax
from jax.experimental import pallas as pl
from jax.experimental.pallas import tpu as pltpu
from jax.sharding import PartitionSpec as P

ORDER = 10
HALO = 16
WIDE = 128
PACK = 64
F32 = jnp.float32
BF16 = jnp.bfloat16
NT = (((1,), (1,)), ((), ()))
NN = (((1,), (0,)), ((), ()))


def degree_signs(coefs):
    index = lax.broadcasted_iota(jnp.int32, (1, coefs), 1)
    degree = jnp.zeros((1, coefs), jnp.int32)
    for level in range(1, ORDER + 1):
        degree = degree + (index >= level * level).astype(jnp.int32)
    return (1 - 2 * (degree % 2)).astype(F32)


def two_terms(value):
    high = value.astype(BF16)
    return high, (value - high.astype(F32)).astype(BF16)


def both_terms(value, axis):
    return jnp.concatenate(two_terms(value), axis=axis)


def dot(left, right, dims):
    return lax.dot_general(left, right, dims, preferred_element_type=F32)


def dot_exact(left, right, dims):
    return lax.dot_general(
        left, right, dims, precision=lax.Precision.HIGHEST, preferred_element_type=F32
    )


def halves(value):
    return value[:, :WIDE] + value[:, WIDE:]


def as_columns(row):
    return jnp.transpose(jnp.broadcast_to(row, (WIDE, row.shape[1])))


def source_indicator(row, cells):
    columns = as_columns(row)
    parts = []
    for at in range(0, cells, WIDE):
        lane = lax.broadcasted_iota(jnp.int32, columns.shape, 1).astype(F32) + float(at)
        parts.append(jnp.where(columns == lane, 1.0, 0.0).astype(BF16))
    return jnp.concatenate(parts, axis=1)


def target_indicator(row, cells):
    shape = (cells, row.shape[1])
    cell = lax.broadcasted_iota(jnp.int32, shape, 0).astype(F32)
    return jnp.where(jnp.broadcast_to(row, shape) == cell, 1.0, 0.0).astype(BF16)


def translate(columns, operator):
    high, low = two_terms(columns)
    op_high, op_low = two_terms(operator)
    return (
        dot(high, op_high, NT) + dot(low, op_high, NT) + dot(high, op_low, NT)
    )


def inner_kernel(window_ref, source_ref, target_ref, operator_ref, out_ref, moved, total):
    offsets = operator_ref.shape[0]
    cells = out_ref.shape[0]
    span = window_ref.shape[1]
    slots = source_ref.shape[1]
    rows = source_ref.shape[0]
    each = rows * slots // offsets
    window = both_terms(window_ref[...], 0)
    for r in range(rows):
        picked = dot(source_indicator(source_ref[r : r + 1, :], span), window, NT)
        moved[r * slots : (r + 1) * slots, :] = halves(picked)
    total[...] = jnp.zeros_like(total)
    for r in range(rows):
        terms = []
        for o in range(r * slots // each, (r + 1) * slots // each):
            terms.append(translate(moved[o * each : (o + 1) * each, :], operator_ref[o]))
        terms = jnp.concatenate(terms, axis=0)
        total[...] += dot(target_indicator(target_ref[r : r + 1, :], cells), both_terms(terms, 1), NN)
    out_ref[...] = halves(total[...])


def far_kernel(top_ref, weight_ref, far_ref, shift_ref, place_ref, near_ref, out_ref):
    top = jnp.concatenate([top_ref[:, 0][:, :, None], top_ref[:, 1][:, :, None]], axis=2)
    top = top.reshape(-1, WIDE)
    summed = dot_exact(weight_ref[...], top, NN)
    parent = dot_exact(summed, far_ref[...], NT)
    table = jnp.concatenate(
        [dot_exact(parent, shift_ref[o], NT) for o in range(shift_ref.shape[0])], axis=0
    )
    table = both_terms(table, 1)
    cells = near_ref.shape[0]
    slots = 128
    for at in range(0, cells, slots):
        picked = dot(source_indicator(place_ref[:, at : at + slots], table.shape[0]), table, NN)
        out_ref[at : at + slots, :] = near_ref[at : at + slots, :] + halves(picked)


def positions(ids):
    slots = ids.shape[1]
    used = ids >= 0.0
    row = lax.broadcasted_iota(jnp.int32, (slots, slots), 0)
    lane = lax.broadcasted_iota(jnp.int32, (slots, slots), 1)
    earlier = jnp.where(row < lane, 1.0, 0.0).astype(BF16)
    place = dot(jnp.where(used, 1.0, 0.0).astype(BF16), earlier, NN)
    return jnp.where(used, place, -1.0)


def digits(ids):
    value = ids + 1.0
    high = jnp.floor(value * (1.0 / 32.0))
    return high, value - 32.0 * high


def translate_and_pack(cells_ref, by_offset_ref, ids, operator_ref, block, terms, signed, store):
    coefs, cells = cells_ref.shape
    offsets = operator_ref.shape[0]
    peers = ids.shape[0]
    sign = degree_signs(WIDE)
    block[...] = jnp.zeros_like(block)
    block[:coefs, :] = cells_ref[...]
    held = both_terms(block[...], 0)
    for o in range(offsets):
        picked = halves(dot(source_indicator(by_offset_ref[o : o + 1, :], cells), held, NT))
        if signed:
            picked = picked * sign
        moved = translate(picked, operator_ref[o])
        if signed:
            moved = moved * sign
        terms[:, o] = moved.reshape(peers, -1, WIDE)
    place = positions(ids)
    high, low = digits(ids)
    packed = []
    for p in range(peers):
        pick = target_indicator(place[p : p + 1, :], PACK)
        store(p, halves(dot(pick, both_terms(terms[p].reshape(-1, WIDE), 1), NN)))
        both = jnp.concatenate([high[p : p + 1], low[p : p + 1]], axis=0).astype(BF16)
        both = dot(both, pick, NT)
        packed.append(32.0 * both[:1] + both[1:] - 1.0)
    return jnp.concatenate(packed, axis=0)


def listed_kernel(cells_ref, by_offset_ref, ids_ref, operator_ref, out_ref, packed_ref, block, terms):
    def store(p, value):
        out_ref[p] = value

    packed_ref[...] = translate_and_pack(
        cells_ref, by_offset_ref, ids_ref[...], operator_ref, block, terms, False, store
    )


def answer_kernel(
    cells_ref, by_offset_ref, ids_ref, operator_ref, listed_ref, listed_ids_ref, out_ref, packed_ref, block, terms
):
    def store(p, value):
        out_ref[p, :PACK] = listed_ref[p]
        out_ref[p, PACK:] = value

    packed = translate_and_pack(
        cells_ref, by_offset_ref, ids_ref[...], operator_ref, block, terms, True, store
    )
    packed_ref[...] = jnp.concatenate([packed, listed_ids_ref[...]], axis=1)


def sum_kernel(terms_ref, target_ref, near_ref, out_ref, total):
    coefs, cells = out_ref.shape
    peers = terms_ref.shape[0]
    total[...] = jnp.zeros_like(total)
    for p in range(0, peers, 2):
        terms = jnp.concatenate([terms_ref[p], terms_ref[p + 1]], axis=0)
        target = jnp.concatenate([target_ref[p : p + 1, :], target_ref[p + 1 : p + 2, :]], axis=1)
        total[...] += dot(target_indicator(target, cells), both_terms(terms, 1), NN)
    result = near_ref[...] + halves(total[...])
    out_ref[...] = jnp.transpose(result)[:coefs, :]


def body(
    multipoles,
    top_multipoles,
    translators,
    child_shifts,
    far_operator,
    far_weights,
    cell_codes,
    inner_sources,
    inner_targets,
    pair_sources,
    peer_target_cells,
    pair_counts,
):
    coefs, cells = multipoles.shape
    parents = far_weights.shape[0]
    peers, offsets, room = pair_sources.shape[1:]
    slots = offsets * room
    pad = WIDE - coefs
    segs = lax.axis_size("seg")
    params = pltpu.CompilerParams(vmem_limit_bytes=48 * 1024 * 1024)

    used = lax.broadcasted_iota(jnp.int32, (peers, offsets, room), 2) < pair_counts[0][..., None]
    own_target = jnp.where(used, peer_target_cells[0], -1).reshape(peers, slots).astype(F32)
    top = jnp.broadcast_to(jnp.pad(top_multipoles[:, 0], (0, pad))[None], (peers, WIDE))
    message = jnp.stack([own_target, top], axis=1)
    arrived = lax.all_to_all(message, "sub", split_axis=0, concat_axis=0, tiled=True)
    their_target, tops = arrived[:, 0], arrived[:, 1]

    ys = 1
    while ys * ys < segs:
        ys *= 2
    xs = segs // ys
    core = lax.axis_index("sub") % 2
    half = peers // 2
    mine = lax.dynamic_slice_in_dim(tops, core * half, half, axis=0)
    spread = lax.all_to_all(
        jnp.broadcast_to(mine[None], (ys, half, WIDE)),
        "seg",
        split_axis=0,
        concat_axis=0,
        tiled=True,
        axis_index_groups=[[x * ys + y for y in range(ys)] for x in range(xs)],
    )
    shared = lax.all_gather(
        spread,
        "sub",
        axis=0,
        tiled=True,
        axis_index_groups=[[2 * i, 2 * i + 1] for i in range(half)],
    )

    up = [(i, i + 1) for i in range(segs - 1)]
    down = [(j, i) for i, j in up]
    before = lax.ppermute(multipoles[:, cells - HALO :], "seg", up)
    after = lax.ppermute(multipoles[:, :HALO], "seg", down)
    window = jnp.concatenate([before, multipoles, after], axis=1)
    span = cells + WIDE
    window = jnp.pad(window, ((0, pad), (0, span - window.shape[1])))

    operators = jnp.pad(translators, ((0, 0), (0, pad), (0, pad)))

    def by_offset(ids):
        return ids.reshape(peers, offsets, room).transpose(1, 0, 2).reshape(offsets, -1)

    own_source = jnp.where(used, pair_sources[0], -1).reshape(peers, slots).astype(F32)
    scratch = [pltpu.VMEM((WIDE, cells), F32), pltpu.VMEM((peers, offsets, room, WIDE), F32)]
    pair_cost = pl.CostEstimate(flops=4 * 10**9, bytes_accessed=3 * 10**6, transcendentals=0)
    listed, listed_ids = pl.pallas_call(
        listed_kernel,
        out_shape=(
            jax.ShapeDtypeStruct((peers, PACK, WIDE), F32),
            jax.ShapeDtypeStruct((peers, PACK), F32),
        ),
        scratch_shapes=scratch,
        compiler_params=params,
        cost_estimate=pair_cost,
        name="listed_terms",
    )(multipoles, by_offset(own_source), own_source, operators)
    packet, targets = pl.pallas_call(
        answer_kernel,
        out_shape=(
            jax.ShapeDtypeStruct((peers, 2 * PACK, WIDE), F32),
            jax.ShapeDtypeStruct((peers, 2 * PACK), F32),
        ),
        scratch_shapes=scratch,
        compiler_params=params,
        cost_estimate=pair_cost,
        name="answers",
    )(multipoles, by_offset(their_target), their_target, operators, listed, listed_ids)
    packet, shared = lax.optimization_barrier((packet, shared))
    received = lax.all_to_all(packet, "sub", split_axis=0, concat_axis=0, tiled=True)

    every_top = shared.reshape(1, 2 * ys * half, WIDE)
    if xs > 1:
        every_top = lax.all_gather(
            every_top,
            "seg",
            axis=0,
            tiled=True,
            axis_index_groups=[[x * ys + y for x in range(xs)] for y in range(ys)],
        )
    every_top = every_top.reshape(xs, 2, ys, half, WIDE)

    shifts = jnp.pad(child_shifts, ((0, 0), (0, pad), (0, pad)))
    far = jnp.pad(far_operator, ((0, pad), (0, pad)))

    inner_rows = inner_sources.shape[1] * inner_sources.shape[2] // 128
    near = pl.pallas_call(
        inner_kernel,
        out_shape=jax.ShapeDtypeStruct((cells, WIDE), F32),
        scratch_shapes=[
            pltpu.VMEM((inner_rows * 128, WIDE), F32),
            pltpu.VMEM((cells, 2 * WIDE), F32),
        ],
        compiler_params=params,
        cost_estimate=pl.CostEstimate(flops=2 * 10**9, bytes_accessed=3 * 10**6, transcendentals=0),
        name="inner_pairs",
    )(
        window,
        inner_sources[0].reshape(inner_rows, 128).astype(F32),
        inner_targets[0].reshape(inner_rows, 128).astype(F32),
        operators,
    )

    octants = child_shifts.shape[0]
    place = (cell_codes % octants * parents + cell_codes // octants).astype(F32)
    near = pl.pallas_call(
        far_kernel,
        out_shape=jax.ShapeDtypeStruct((cells, WIDE), F32),
        compiler_params=params,
        cost_estimate=pl.CostEstimate(flops=10**9, bytes_accessed=2 * 10**6, transcendentals=0),
        name="far_field",
    )(every_top, far_weights, far, shifts, place, near)

    return pl.pallas_call(
        sum_kernel,
        out_shape=jax.ShapeDtypeStruct((coefs, cells), F32),
        scratch_shapes=[pltpu.VMEM((cells, 2 * WIDE), F32)],
        compiler_params=params,
        cost_estimate=pl.CostEstimate(flops=2 * 10**9, bytes_accessed=3 * 10**6, transcendentals=0),
        name="sum_terms",
    )(received, targets, near)


def solution(mesh):
    in_specs = (
        P(None, ("seg", "sub")),
        P(None, ("seg", "sub")),
        P(),
        P(),
        P(),
        P(("seg", "sub"), None),
        P(("seg", "sub"), None),
        P(("seg", "sub"), None, None),
        P(("seg", "sub"), None, None),
        P(("seg", "sub"), None, None, None),
        P(("seg", "sub"), None, None, None),
        P(("seg", "sub"), None, None),
    )
    out_specs = P(None, ("seg", "sub"))
    return jax.shard_map(body, mesh=mesh, in_specs=in_specs, out_specs=out_specs, check_vma=False)
```

```python
import jax
import jax.numpy as jnp
from jax import lax
from jax.experimental import pallas as pl
from jax.experimental.pallas import tpu as pltpu
from jax.sharding import PartitionSpec as P

ORDER = 10
HALO = 16
WIDE = 128
PACK = 64
F32 = jnp.float32
BF16 = jnp.bfloat16
NT = (((1,), (1,)), ((), ()))
NN = (((1,), (0,)), ((), ()))


def degree_signs(coefs):
    index = lax.broadcasted_iota(jnp.int32, (1, coefs), 1)
    degree = jnp.zeros((1, coefs), jnp.int32)
    for level in range(1, ORDER + 1):
        degree = degree + (index >= level * level).astype(jnp.int32)
    return (1 - 2 * (degree % 2)).astype(F32)


def two_terms(value):
    high = value.astype(BF16)
    return high, (value - high.astype(F32)).astype(BF16)


def both_terms(value, axis):
    return jnp.concatenate(two_terms(value), axis=axis)


def dot(left, right, dims):
    return lax.dot_general(left, right, dims, preferred_element_type=F32)


def dot_exact(left, right, dims):
    return lax.dot_general(
        left, right, dims, precision=lax.Precision.HIGHEST, preferred_element_type=F32
    )


def halves(value):
    return value[:, :WIDE] + value[:, WIDE:]


def as_columns(row):
    return jnp.transpose(jnp.broadcast_to(row, (WIDE, row.shape[1])))


def source_indicator(row, cells):
    columns = as_columns(row)
    parts = []
    for at in range(0, cells, WIDE):
        lane = lax.broadcasted_iota(jnp.int32, columns.shape, 1).astype(F32) + float(at)
        parts.append(jnp.where(columns == lane, 1.0, 0.0).astype(BF16))
    return jnp.concatenate(parts, axis=1)


def target_indicator(row, cells):
    shape = (cells, row.shape[1])
    cell = lax.broadcasted_iota(jnp.int32, shape, 0).astype(F32)
    return jnp.where(jnp.broadcast_to(row, shape) == cell, 1.0, 0.0).astype(BF16)


def translate(columns, operator):
    high, low = two_terms(columns)
    return dot(jnp.concatenate([high, low, high], axis=1), operator, NN)


def three_terms(operators):
    pad = WIDE - operators.shape[1]
    turned = jnp.pad(jnp.swapaxes(operators, 1, 2), ((0, 0), (0, pad), (0, pad)))
    high = lax.reduce_precision(turned, 8, 7)
    return jnp.concatenate([high, high, turned - high], axis=1).astype(BF16)


def turned_terms(block):
    return both_terms(jnp.transpose(block), 1)


def inner_kernel(window_ref, source_ref, target_ref, operator_ref, out_ref, moved, total):
    offsets = operator_ref.shape[0]
    cells = out_ref.shape[0]
    span = window_ref.shape[1]
    slots = source_ref.shape[1]
    rows = source_ref.shape[0]
    each = rows * slots // offsets
    window = turned_terms(window_ref[...])
    for r in range(rows):
        picked = dot(source_indicator(source_ref[r : r + 1, :], span), window, NN)
        moved[r * slots : (r + 1) * slots, :] = halves(picked)
    total[...] = jnp.zeros_like(total)
    for r in range(rows):
        terms = []
        for o in range(r * slots // each, (r + 1) * slots // each):
            terms.append(translate(moved[o * each : (o + 1) * each, :], operator_ref[o]))
        terms = jnp.concatenate(terms, axis=0)
        total[...] += dot(target_indicator(target_ref[r : r + 1, :], cells), both_terms(terms, 1), NN)
    out_ref[...] = halves(total[...])


def far_kernel(top_ref, weight_ref, far_ref, shift_ref, place_ref, near_ref, out_ref):
    top = jnp.concatenate([top_ref[0][:, None], top_ref[1][:, None]], axis=1)
    top = top.reshape(-1, WIDE)
    summed = dot_exact(weight_ref[...], top, NN)
    parent = dot_exact(summed, far_ref[...], NT)
    table = jnp.concatenate(
        [dot_exact(parent, shift_ref[o], NT) for o in range(shift_ref.shape[0])], axis=0
    )
    table = both_terms(table, 1)
    cells = near_ref.shape[0]
    slots = 128
    for at in range(0, cells, slots):
        picked = dot(source_indicator(place_ref[:, at : at + slots], table.shape[0]), table, NN)
        out_ref[at : at + slots, :] = near_ref[at : at + slots, :] + halves(picked)


def positions(ids):
    slots = ids.shape[1]
    used = ids >= 0.0
    row = lax.broadcasted_iota(jnp.int32, (slots, slots), 0)
    lane = lax.broadcasted_iota(jnp.int32, (slots, slots), 1)
    earlier = jnp.where(row < lane, 1.0, 0.0).astype(BF16)
    place = dot(jnp.where(used, 1.0, 0.0).astype(BF16), earlier, NN)
    return jnp.where(used, place, -1.0)


def translate_and_pack(cells_ref, by_offset_ref, ids_ref, operator_ref, block, picked, terms, signed, store):
    coefs, cells = cells_ref.shape
    offsets, slots = by_offset_ref.shape
    peers = ids_ref.shape[0]
    sign = degree_signs(WIDE)
    block[coefs // 8 * 8 :, :] = jnp.zeros((WIDE - coefs // 8 * 8, cells), F32)
    block[:coefs, :] = cells_ref[...]
    held = turned_terms(block[...])
    for o in range(0, offsets, 2):
        chosen = jnp.concatenate(
            [source_indicator(by_offset_ref[i : i + 1, :], cells) for i in (o, o + 1)], axis=0
        )
        columns = halves(dot(chosen, held, NN))
        picked[o * slots : (o + 2) * slots, :] = columns * sign if signed else columns
    for o in range(offsets):
        moved = translate(picked[o * slots : (o + 1) * slots, :], operator_ref[o])
        terms[:, o] = (moved * sign if signed else moved).reshape(peers, -1, WIDE)
    place = positions(ids_ref[...])
    for p in range(peers):
        pick = target_indicator(place[p : p + 1, :], PACK)
        store(p, halves(dot(pick, both_terms(terms[p].reshape(-1, WIDE), 1), NN)))


def listed_kernel(cells_ref, by_offset_ref, ids_ref, operator_ref, out_ref, block, picked, terms):
    def store(p, value):
        out_ref[p] = value

    translate_and_pack(
        cells_ref, by_offset_ref, ids_ref, operator_ref, block, picked, terms, False, store
    )


def answer_kernel(
    cells_ref, by_offset_ref, ids_ref, operator_ref, listed_ref, out_ref, block, picked, terms
):
    def store(p, value):
        out_ref[p, :PACK] = listed_ref[p]
        out_ref[p, PACK:] = value

    translate_and_pack(
        cells_ref, by_offset_ref, ids_ref, operator_ref, block, picked, terms, True, store
    )


def pack_ids(ids):
    place = positions(ids)
    value = ids + 1.0
    high = jnp.floor(value * (1.0 / 32.0))
    low = value - 32.0 * high
    packed = []
    for p in range(ids.shape[0]):
        pick = target_indicator(place[p : p + 1, :], PACK)
        both = jnp.concatenate([high[p : p + 1], low[p : p + 1]], axis=0).astype(BF16)
        both = dot(both, pick, NT)
        packed.append(32.0 * both[:1] + both[1:] - 1.0)
    return jnp.concatenate(packed, axis=0)


def target_kernel(their_ref, own_ref, out_ref):
    out_ref[...] = jnp.concatenate([pack_ids(their_ref[...]), pack_ids(own_ref[...])], axis=1)


def spread_ids(ids, counts):
    peers, offsets, room = ids.shape
    slots = offsets * room
    value = ids.reshape(peers * offsets, room).astype(F32)
    high = jnp.floor(value * (1.0 / 32.0))
    both = jnp.concatenate([high, value - 32.0 * high], axis=0).astype(BF16)
    row = lax.broadcasted_iota(jnp.int32, (room, slots), 0)
    lane = lax.broadcasted_iota(jnp.int32, (room, slots), 1)
    wide = dot(both, jnp.where(lane % room == row, 1.0, 0.0).astype(BF16), NN)
    wide = 32.0 * wide[: peers * offsets] + wide[peers * offsets :]
    wide = wide.reshape(peers, offsets, slots)
    row = lax.broadcasted_iota(jnp.int32, wide.shape, 1)
    lane = lax.broadcasted_iota(jnp.int32, wide.shape, 2)
    flat = jnp.sum(jnp.where(lane // room == row, wide, 0.0), axis=1)
    row = lax.broadcasted_iota(jnp.int32, (offsets, slots), 0)
    lane = lax.broadcasted_iota(jnp.int32, (offsets, slots), 1)
    count = dot(counts.astype(F32).astype(BF16), jnp.where(lane // room == row, 1.0, 0.0).astype(BF16), NN)
    slot = lax.broadcasted_iota(jnp.int32, flat.shape, 1) % room
    return jnp.where(slot.astype(F32) < count, flat, -1.0)


def message_kernel(source_ref, target_ref, count_ref, top_ref, out_ref, own_source_ref):
    peers = target_ref.shape[0]
    counts = count_ref[...]
    coefs = top_ref.shape[1]
    own_source_ref[...] = spread_ids(source_ref[...], counts)
    own_target = spread_ids(target_ref[...], counts)
    out_ref[:, 1, :coefs] = jnp.broadcast_to(top_ref[...], (peers, coefs))
    out_ref[:, 1, coefs:] = jnp.zeros((peers, WIDE - coefs), F32)
    out_ref[:, 0, :] = own_target


def sum_kernel(terms_ref, target_ref, near_ref, out_ref, total):
    coefs, cells = out_ref.shape
    peers = terms_ref.shape[0]
    total[...] = jnp.zeros_like(total)
    for p in range(0, peers, 2):
        terms = jnp.concatenate([terms_ref[p], terms_ref[p + 1]], axis=0)
        target = jnp.concatenate([target_ref[p : p + 1, :], target_ref[p + 1 : p + 2, :]], axis=1)
        total[...] += dot(target_indicator(target, cells), both_terms(terms, 1), NN)
    result = near_ref[...] + halves(total[...])
    out_ref[...] = jnp.transpose(result)[:coefs, :]


def body(
    multipoles,
    top_multipoles,
    translators,
    child_shifts,
    far_operator,
    far_weights,
    cell_codes,
    inner_sources,
    inner_targets,
    pair_sources,
    peer_target_cells,
    pair_counts,
):
    coefs, cells = multipoles.shape
    parents = far_weights.shape[0]
    peers, offsets, room = pair_sources.shape[1:]
    slots = offsets * room
    pad = WIDE - coefs
    segs = lax.axis_size("seg")
    params = pltpu.CompilerParams(vmem_limit_bytes=48 * 1024 * 1024)

    message, own_source = pl.pallas_call(
        message_kernel,
        out_shape=(
            jax.ShapeDtypeStruct((peers, 2, WIDE), F32),
            jax.ShapeDtypeStruct((peers, slots), F32),
        ),
        compiler_params=params,
        name="message",
    )(pair_sources[0], peer_target_cells[0], pair_counts[0], top_multipoles.reshape(1, coefs))
    arrived = lax.all_to_all(message, "sub", split_axis=0, concat_axis=0, tiled=True)
    their_target, tops = arrived[:, 0], arrived[:, 1]

    core = lax.axis_index("sub") % 2
    half = peers // 2
    mine = lax.dynamic_slice_in_dim(tops, core * half, half, axis=0)
    spread = lax.all_to_all(
        jnp.broadcast_to(mine[None], (segs, half, WIDE)), "seg", split_axis=0, concat_axis=0, tiled=True
    )

    up = [(i, i + 1) for i in range(segs - 1)]
    down = [(j, i) for i, j in up]
    before = lax.ppermute(multipoles[:, cells - HALO :], "seg", up)
    after = lax.ppermute(multipoles[:, :HALO], "seg", down)
    window = jnp.concatenate([before, multipoles, after], axis=1)
    span = cells + WIDE
    window = jnp.pad(window, ((0, pad), (0, span - window.shape[1])))

    operators = three_terms(translators)

    def by_offset(ids):
        return ids.reshape(peers, offsets, room).transpose(1, 0, 2).reshape(offsets, -1)

    scratch = [
        pltpu.VMEM((WIDE, cells), F32),
        pltpu.VMEM((offsets * peers * room, WIDE), F32),
        pltpu.VMEM((peers, offsets, room, WIDE), F32),
    ]
    pair_cost = pl.CostEstimate(flops=2 * 10**9, bytes_accessed=3 * 10**6, transcendentals=0)
    listed = pl.pallas_call(
        listed_kernel,
        out_shape=jax.ShapeDtypeStruct((peers, PACK, WIDE), F32),
        scratch_shapes=scratch,
        compiler_params=params,
        cost_estimate=pair_cost,
        name="listed_terms",
    )(multipoles, by_offset(own_source), own_source, operators)
    packet = pl.pallas_call(
        answer_kernel,
        out_shape=jax.ShapeDtypeStruct((peers, 2 * PACK, WIDE), F32),
        scratch_shapes=scratch,
        compiler_params=params,
        cost_estimate=pair_cost,
        name="answers",
    )(multipoles, by_offset(their_target), their_target, operators, listed)
    packet, spread = lax.optimization_barrier((packet, spread))
    received = lax.all_to_all(packet, "sub", split_axis=0, concat_axis=0, tiled=True)
    every_top = lax.all_gather(
        spread,
        "sub",
        axis=0,
        tiled=False,
        axis_index_groups=[[2 * i, 2 * i + 1] for i in range(half)],
    )
    targets = pl.pallas_call(
        target_kernel,
        out_shape=jax.ShapeDtypeStruct((peers, 2 * PACK), F32),
        compiler_params=params,
        name="packed_targets",
    )(their_target, own_source)

    shifts = jnp.pad(child_shifts, ((0, 0), (0, pad), (0, pad)))
    far = jnp.pad(far_operator, ((0, pad), (0, pad)))

    inner_rows = inner_sources.shape[1] * inner_sources.shape[2] // 128
    near = pl.pallas_call(
        inner_kernel,
        out_shape=jax.ShapeDtypeStruct((cells, WIDE), F32),
        scratch_shapes=[
            pltpu.VMEM((inner_rows * 128, WIDE), F32),
            pltpu.VMEM((cells, 2 * WIDE), F32),
        ],
        compiler_params=params,
        cost_estimate=pl.CostEstimate(flops=2 * 10**9, bytes_accessed=3 * 10**6, transcendentals=0),
        name="inner_pairs",
    )(
        window,
        inner_sources[0].reshape(inner_rows, 128).astype(F32),
        inner_targets[0].reshape(inner_rows, 128).astype(F32),
        operators,
    )

    octants = child_shifts.shape[0]
    place = (cell_codes % octants * parents + cell_codes // octants).astype(F32)
    near = pl.pallas_call(
        far_kernel,
        out_shape=jax.ShapeDtypeStruct((cells, WIDE), F32),
        compiler_params=params,
        cost_estimate=pl.CostEstimate(flops=10**9, bytes_accessed=2 * 10**6, transcendentals=0),
        name="far_field",
    )(every_top, far_weights, far, shifts, place, near)

    return pl.pallas_call(
        sum_kernel,
        out_shape=jax.ShapeDtypeStruct((coefs, cells), F32),
        scratch_shapes=[pltpu.VMEM((cells, 2 * WIDE), F32)],
        compiler_params=params,
        cost_estimate=pl.CostEstimate(flops=2 * 10**9, bytes_accessed=3 * 10**6, transcendentals=0),
        name="sum_terms",
    )(received, targets, near)


def solution(mesh):
    in_specs = (
        P(None, ("seg", "sub")),
        P(None, ("seg", "sub")),
        P(),
        P(),
        P(),
        P(("seg", "sub"), None),
        P(("seg", "sub"), None),
        P(("seg", "sub"), None, None),
        P(("seg", "sub"), None, None),
        P(("seg", "sub"), None, None, None),
        P(("seg", "sub"), None, None, None),
        P(("seg", "sub"), None, None),
    )
    out_specs = P(None, ("seg", "sub"))
    return jax.shard_map(body, mesh=mesh, in_specs=in_specs, out_specs=out_specs, check_vma=False)
```

```python
import jax
import jax.numpy as jnp
from jax import lax
from jax.experimental import pallas as pl
from jax.experimental.pallas import tpu as pltpu
from jax.sharding import PartitionSpec as P

ORDER = 10
HALO = 16
WIDE = 128
PACK = 64
F32 = jnp.float32
BF16 = jnp.bfloat16
NT = (((1,), (1,)), ((), ()))
NN = (((1,), (0,)), ((), ()))


def degree_signs(coefs):
    index = lax.broadcasted_iota(jnp.int32, (1, coefs), 1)
    degree = jnp.zeros((1, coefs), jnp.int32)
    for level in range(1, ORDER + 1):
        degree = degree + (index >= level * level).astype(jnp.int32)
    return (1 - 2 * (degree % 2)).astype(F32)


def two_terms(value):
    high = value.astype(BF16)
    return high, (value - high.astype(F32)).astype(BF16)


def both_terms(value, axis):
    return jnp.concatenate(two_terms(value), axis=axis)


def dot(left, right, dims):
    return lax.dot_general(left, right, dims, preferred_element_type=F32)


def dot_exact(left, right, dims):
    return lax.dot_general(
        left, right, dims, precision=lax.Precision.HIGHEST, preferred_element_type=F32
    )


def halves(value):
    return value[:, :WIDE] + value[:, WIDE:]


def as_columns(row):
    return jnp.transpose(jnp.broadcast_to(row, (WIDE, row.shape[1])))


def source_indicator(row, cells):
    columns = as_columns(row)
    parts = []
    for at in range(0, cells, WIDE):
        lane = lax.broadcasted_iota(jnp.int32, columns.shape, 1).astype(F32) + float(at)
        parts.append(jnp.where(columns == lane, 1.0, 0.0).astype(BF16))
    return jnp.concatenate(parts, axis=1)


def target_indicator(row, cells):
    shape = (cells, row.shape[1])
    cell = lax.broadcasted_iota(jnp.int32, shape, 0).astype(F32)
    return jnp.where(jnp.broadcast_to(row, shape) == cell, 1.0, 0.0).astype(BF16)


def translate(columns, operator):
    high, low = two_terms(columns)
    return dot(jnp.concatenate([high, low, high], axis=1), operator, NN)


def three_terms(operators):
    pad = WIDE - operators.shape[1]
    turned = jnp.pad(jnp.swapaxes(operators, 1, 2), ((0, 0), (0, pad), (0, pad)))
    high = lax.reduce_precision(turned, 8, 7)
    return jnp.concatenate([high, high, turned - high], axis=1).astype(BF16)


def turned_terms(block):
    return both_terms(jnp.transpose(block), 1)


def inner_kernel(window_ref, source_ref, target_ref, operator_ref, out_ref, moved, total):
    offsets = operator_ref.shape[0]
    cells = out_ref.shape[0]
    span = window_ref.shape[1]
    slots = source_ref.shape[1]
    rows = source_ref.shape[0]
    each = rows * slots // offsets
    window = turned_terms(window_ref[...])
    for r in range(rows):
        picked = dot(source_indicator(source_ref[r : r + 1, :], span), window, NN)
        moved[r * slots : (r + 1) * slots, :] = halves(picked)
    total[...] = jnp.zeros_like(total)
    for r in range(rows):
        terms = []
        for o in range(r * slots // each, (r + 1) * slots // each):
            terms.append(translate(moved[o * each : (o + 1) * each, :], operator_ref[o]))
        terms = jnp.concatenate(terms, axis=0)
        total[...] += dot(target_indicator(target_ref[r : r + 1, :], cells), both_terms(terms, 1), NN)
    out_ref[...] = halves(total[...])


def far_kernel(top_ref, weight_ref, far_ref, shift_ref, place_ref, near_ref, out_ref):
    top = jnp.concatenate([top_ref[0][:, None], top_ref[1][:, None]], axis=1)
    top = top.reshape(-1, WIDE)
    summed = dot_exact(weight_ref[...], top, NN)
    parent = dot_exact(summed, far_ref[...], NT)
    table = jnp.concatenate(
        [dot_exact(parent, shift_ref[o], NT) for o in range(shift_ref.shape[0])], axis=0
    )
    table = both_terms(table, 1)
    cells = near_ref.shape[0]
    slots = 128
    for at in range(0, cells, slots):
        picked = dot(source_indicator(place_ref[:, at : at + slots], table.shape[0]), table, NN)
        out_ref[at : at + slots, :] = near_ref[at : at + slots, :] + halves(picked)


def positions(ids):
    slots = ids.shape[1]
    used = ids >= 0.0
    row = lax.broadcasted_iota(jnp.int32, (slots, slots), 0)
    lane = lax.broadcasted_iota(jnp.int32, (slots, slots), 1)
    earlier = jnp.where(row < lane, 1.0, 0.0).astype(BF16)
    place = dot(jnp.where(used, 1.0, 0.0).astype(BF16), earlier, NN)
    return jnp.where(used, place, -1.0)


def translate_and_pack(cells_ref, by_offset_ref, ids_ref, operator_ref, block, picked, terms, signed, store):
    coefs, cells = cells_ref.shape
    offsets, slots = by_offset_ref.shape
    peers = ids_ref.shape[0]
    sign = degree_signs(WIDE)
    block[coefs // 8 * 8 :, :] = jnp.zeros((WIDE - coefs // 8 * 8, cells), F32)
    block[:coefs, :] = cells_ref[...]
    held = turned_terms(block[...])
    for o in range(0, offsets, 2):
        chosen = jnp.concatenate(
            [source_indicator(by_offset_ref[i : i + 1, :], cells) for i in (o, o + 1)], axis=0
        )
        columns = halves(dot(chosen, held, NN))
        picked[o * slots : (o + 2) * slots, :] = columns * sign if signed else columns
    for o in range(offsets):
        moved = translate(picked[o * slots : (o + 1) * slots, :], operator_ref[o])
        terms[:, o] = (moved * sign if signed else moved).reshape(peers, -1, WIDE)
    place = positions(ids_ref[...])
    for p in range(peers):
        pick = target_indicator(place[p : p + 1, :], PACK)
        store(p, halves(dot(pick, both_terms(terms[p].reshape(-1, WIDE), 1), NN)))


def listed_kernel(cells_ref, by_offset_ref, ids_ref, operator_ref, out_ref, block, picked, terms):
    def store(p, value):
        out_ref[p] = value

    translate_and_pack(
        cells_ref, by_offset_ref, ids_ref, operator_ref, block, picked, terms, False, store
    )


def answer_kernel(
    cells_ref, by_offset_ref, ids_ref, operator_ref, listed_ref, out_ref, block, picked, terms
):
    def store(p, value):
        out_ref[p, :PACK] = listed_ref[p]
        out_ref[p, PACK:] = value

    translate_and_pack(
        cells_ref, by_offset_ref, ids_ref, operator_ref, block, picked, terms, True, store
    )


def pack_ids(ids):
    place = positions(ids)
    value = ids + 1.0
    high = jnp.floor(value * (1.0 / 32.0))
    low = value - 32.0 * high
    packed = []
    for p in range(ids.shape[0]):
        pick = target_indicator(place[p : p + 1, :], PACK)
        both = jnp.concatenate([high[p : p + 1], low[p : p + 1]], axis=0).astype(BF16)
        both = dot(both, pick, NT)
        packed.append(32.0 * both[:1] + both[1:] - 1.0)
    return jnp.concatenate(packed, axis=0)


def target_kernel(their_ref, own_ref, out_ref):
    out_ref[...] = jnp.concatenate([pack_ids(their_ref[...]), pack_ids(own_ref[...])], axis=1)


def message_kernel(target_ref, count_ref, top_ref, out_ref):
    peers, room, offsets = target_ref.shape
    coefs = top_ref.shape[1]
    counts = count_ref[...]
    for c in range(room):
        ids = jnp.where(c < counts, target_ref[:, c, :], -1).astype(F32)
        out_ref[:, 0, c * offsets : (c + 1) * offsets] = ids
    out_ref[:, 1, :coefs] = jnp.broadcast_to(top_ref[...], (peers, coefs))
    out_ref[:, 1, coefs:] = jnp.zeros((peers, WIDE - coefs), F32)


def sum_kernel(terms_ref, target_ref, near_ref, out_ref, total):
    coefs, cells = out_ref.shape
    peers = terms_ref.shape[0]
    total[...] = jnp.zeros_like(total)
    for p in range(0, peers, 2):
        terms = jnp.concatenate([terms_ref[p], terms_ref[p + 1]], axis=0)
        target = jnp.concatenate([target_ref[p : p + 1, :], target_ref[p + 1 : p + 2, :]], axis=1)
        total[...] += dot(target_indicator(target, cells), both_terms(terms, 1), NN)
    result = near_ref[...] + halves(total[...])
    out_ref[...] = jnp.transpose(result)[:coefs, :]


def body(
    multipoles,
    top_multipoles,
    translators,
    child_shifts,
    far_operator,
    far_weights,
    cell_codes,
    inner_sources,
    inner_targets,
    pair_sources,
    peer_target_cells,
    pair_counts,
):
    coefs, cells = multipoles.shape
    parents = far_weights.shape[0]
    peers, offsets, room = pair_sources.shape[1:]
    slots = offsets * room
    pad = WIDE - coefs
    segs = lax.axis_size("seg")
    params = pltpu.CompilerParams(vmem_limit_bytes=48 * 1024 * 1024)

    message = pl.pallas_call(
        message_kernel,
        out_shape=jax.ShapeDtypeStruct((peers, 2, WIDE), F32),
        name="message",
    )(peer_target_cells[0].transpose(0, 2, 1), pair_counts[0], top_multipoles.reshape(1, coefs))
    arrived = lax.all_to_all(message, "sub", split_axis=0, concat_axis=0, tiled=True)
    their_target, tops = arrived[:, 0].reshape(peers, room, offsets), arrived[:, 1]

    def by_peer(ids):
        return ids.transpose(0, 2, 1).reshape(peers, slots).astype(F32)

    def by_offset(ids):
        return ids.transpose(2, 0, 1).reshape(offsets, -1).astype(F32)

    used = lax.broadcasted_iota(jnp.int32, (peers, room, offsets), 1) < pair_counts[0][:, None, :]
    own_source = jnp.where(used, pair_sources[0].transpose(0, 2, 1), -1)
    operators = three_terms(translators)
    scratch = [
        pltpu.VMEM((WIDE, cells), F32),
        pltpu.VMEM((offsets * peers * room, WIDE), F32),
        pltpu.VMEM((peers, offsets, room, WIDE), F32),
    ]
    pair_cost = pl.CostEstimate(flops=2 * 10**9, bytes_accessed=3 * 10**6, transcendentals=0)
    listed = pl.pallas_call(
        listed_kernel,
        out_shape=jax.ShapeDtypeStruct((peers, PACK, WIDE), F32),
        scratch_shapes=scratch,
        compiler_params=params,
        cost_estimate=pair_cost,
        name="listed_terms",
    )(multipoles, by_offset(own_source), by_peer(own_source), operators)
    tops, listed = lax.optimization_barrier((tops, listed))

    core = lax.axis_index("sub") % 2
    half = peers // 2
    mine = lax.dynamic_slice_in_dim(tops, core * half, half, axis=0)
    spread = lax.all_to_all(
        jnp.broadcast_to(mine[None], (segs, half, WIDE)), "seg", split_axis=0, concat_axis=0, tiled=True
    )

    up = [(i, i + 1) for i in range(segs - 1)]
    down = [(j, i) for i, j in up]
    before = lax.ppermute(multipoles[:, cells - HALO :], "seg", up)
    after = lax.ppermute(multipoles[:, :HALO], "seg", down)
    window = jnp.concatenate([before, multipoles, after], axis=1)
    span = cells + WIDE
    window = jnp.pad(window, ((0, pad), (0, span - window.shape[1])))

    packet = pl.pallas_call(
        answer_kernel,
        out_shape=jax.ShapeDtypeStruct((peers, 2 * PACK, WIDE), F32),
        scratch_shapes=scratch,
        compiler_params=params,
        cost_estimate=pair_cost,
        name="answers",
    )(multipoles, by_offset(their_target), by_peer(their_target), operators, listed)
    packet, spread = lax.optimization_barrier((packet, spread))
    received = lax.all_to_all(packet, "sub", split_axis=0, concat_axis=0, tiled=True)
    every_top = lax.all_gather(
        spread,
        "sub",
        axis=0,
        tiled=False,
        axis_index_groups=[[2 * i, 2 * i + 1] for i in range(half)],
    )
    targets = pl.pallas_call(
        target_kernel,
        out_shape=jax.ShapeDtypeStruct((peers, 2 * PACK), F32),
        compiler_params=params,
        name="packed_targets",
    )(by_peer(their_target), by_peer(own_source))

    shifts = jnp.pad(child_shifts, ((0, 0), (0, pad), (0, pad)))
    far = jnp.pad(far_operator, ((0, pad), (0, pad)))

    inner_rows = inner_sources.shape[1] * inner_sources.shape[2] // 128
    near = pl.pallas_call(
        inner_kernel,
        out_shape=jax.ShapeDtypeStruct((cells, WIDE), F32),
        scratch_shapes=[
            pltpu.VMEM((inner_rows * 128, WIDE), F32),
            pltpu.VMEM((cells, 2 * WIDE), F32),
        ],
        compiler_params=params,
        cost_estimate=pl.CostEstimate(flops=2 * 10**9, bytes_accessed=3 * 10**6, transcendentals=0),
        name="inner_pairs",
    )(
        window,
        inner_sources[0].reshape(inner_rows, 128).astype(F32),
        inner_targets[0].reshape(inner_rows, 128).astype(F32),
        operators,
    )

    octants = child_shifts.shape[0]
    place = (cell_codes % octants * parents + cell_codes // octants).astype(F32)
    near = pl.pallas_call(
        far_kernel,
        out_shape=jax.ShapeDtypeStruct((cells, WIDE), F32),
        compiler_params=params,
        cost_estimate=pl.CostEstimate(flops=10**9, bytes_accessed=2 * 10**6, transcendentals=0),
        name="far_field",
    )(every_top, far_weights, far, shifts, place, near)

    return pl.pallas_call(
        sum_kernel,
        out_shape=jax.ShapeDtypeStruct((coefs, cells), F32),
        scratch_shapes=[pltpu.VMEM((cells, 2 * WIDE), F32)],
        compiler_params=params,
        cost_estimate=pl.CostEstimate(flops=2 * 10**9, bytes_accessed=3 * 10**6, transcendentals=0),
        name="sum_terms",
    )(received, targets, near)


def solution(mesh):
    in_specs = (
        P(None, ("seg", "sub")),
        P(None, ("seg", "sub")),
        P(),
        P(),
        P(),
        P(("seg", "sub"), None),
        P(("seg", "sub"), None),
        P(("seg", "sub"), None, None),
        P(("seg", "sub"), None, None),
        P(("seg", "sub"), None, None, None),
        P(("seg", "sub"), None, None, None),
        P(("seg", "sub"), None, None),
    )
    out_specs = P(None, ("seg", "sub"))
    return jax.shard_map(body, mesh=mesh, in_specs=in_specs, out_specs=out_specs, check_vma=False)
```

```python
import jax
import jax.numpy as jnp
from jax import lax
from jax.experimental import pallas as pl
from jax.experimental.pallas import tpu as pltpu
from jax.sharding import PartitionSpec as P

ORDER = 10
HALO = 16
WIDE = 128
PACK = 64
F32 = jnp.float32
BF16 = jnp.bfloat16
NT = (((1,), (1,)), ((), ()))
NN = (((1,), (0,)), ((), ()))


def degree_signs(coefs):
    index = lax.broadcasted_iota(jnp.int32, (1, coefs), 1)
    degree = jnp.zeros((1, coefs), jnp.int32)
    for level in range(1, ORDER + 1):
        degree = degree + (index >= level * level).astype(jnp.int32)
    return (1 - 2 * (degree % 2)).astype(F32)


def two_terms(value):
    high = value.astype(BF16)
    return high, (value - high.astype(F32)).astype(BF16)


def both_terms(value, axis):
    return jnp.concatenate(two_terms(value), axis=axis)


def dot(left, right, dims):
    return lax.dot_general(left, right, dims, preferred_element_type=F32)


def dot_exact(left, right, dims):
    return lax.dot_general(
        left, right, dims, precision=lax.Precision.HIGHEST, preferred_element_type=F32
    )


def halves(value):
    return value[:, :WIDE] + value[:, WIDE:]


def as_columns(row):
    return jnp.transpose(jnp.broadcast_to(row, (WIDE, row.shape[1])))


def source_indicator(row, cells):
    columns = as_columns(row)
    parts = []
    for at in range(0, cells, WIDE):
        lane = lax.broadcasted_iota(jnp.int32, columns.shape, 1).astype(F32) + float(at)
        parts.append(jnp.where(columns == lane, 1.0, 0.0).astype(BF16))
    return jnp.concatenate(parts, axis=1)


def target_indicator(row, cells):
    shape = (cells, row.shape[1])
    cell = lax.broadcasted_iota(jnp.int32, shape, 0).astype(F32)
    return jnp.where(jnp.broadcast_to(row, shape) == cell, 1.0, 0.0).astype(BF16)


def translate(columns, operator):
    high, low = two_terms(columns)
    return dot(jnp.concatenate([high, low, high], axis=1), operator, NN)


def three_terms(operators):
    pad = WIDE - operators.shape[1]
    turned = jnp.pad(jnp.swapaxes(operators, 1, 2), ((0, 0), (0, pad), (0, pad)))
    high = lax.reduce_precision(turned, 8, 7)
    return jnp.concatenate([high, high, turned - high], axis=1).astype(BF16)


def turned_terms(block):
    return both_terms(jnp.transpose(block), 1)


def inner_kernel(window_ref, source_ref, target_ref, operator_ref, out_ref, moved, total):
    offsets = operator_ref.shape[0]
    cells = out_ref.shape[0]
    span = window_ref.shape[1]
    slots = source_ref.shape[1]
    rows = source_ref.shape[0]
    each = rows * slots // offsets
    window = turned_terms(window_ref[...])
    for r in range(rows):
        picked = dot(source_indicator(source_ref[r : r + 1, :], span), window, NN)
        moved[r * slots : (r + 1) * slots, :] = halves(picked)
    total[...] = jnp.zeros_like(total)
    for r in range(rows):
        terms = []
        for o in range(r * slots // each, (r + 1) * slots // each):
            terms.append(translate(moved[o * each : (o + 1) * each, :], operator_ref[o]))
        terms = jnp.concatenate(terms, axis=0)
        total[...] += dot(target_indicator(target_ref[r : r + 1, :], cells), both_terms(terms, 1), NN)
    out_ref[...] = halves(total[...])


def far_kernel(place_x_ref, top_ref, weight_ref, far_ref, shift_ref, place_ref, near_ref, out_ref):
    xs = top_ref.shape[1]
    top = []
    for x in range(xs):
        ahead = lax.rem(x + place_x_ref[0], min(xs, 2)) * (xs // 2) + x // 2
        both = [top_ref[core, ahead][:, None] for core in (0, 1)]
        top.append(jnp.concatenate(both, axis=1).reshape(-1, WIDE))
    top = jnp.concatenate(top, axis=0)
    summed = dot_exact(weight_ref[...], top, NN)
    parent = dot_exact(summed, far_ref[...], NT)
    table = jnp.concatenate(
        [dot_exact(parent, shift_ref[o], NT) for o in range(shift_ref.shape[0])], axis=0
    )
    table = both_terms(table, 1)
    cells = near_ref.shape[0]
    slots = 128
    for at in range(0, cells, slots):
        picked = dot(source_indicator(place_ref[:, at : at + slots], table.shape[0]), table, NN)
        out_ref[at : at + slots, :] = near_ref[at : at + slots, :] + halves(picked)


def positions(ids):
    slots = ids.shape[1]
    used = ids >= 0.0
    row = lax.broadcasted_iota(jnp.int32, (slots, slots), 0)
    lane = lax.broadcasted_iota(jnp.int32, (slots, slots), 1)
    earlier = jnp.where(row < lane, 1.0, 0.0).astype(BF16)
    place = dot(jnp.where(used, 1.0, 0.0).astype(BF16), earlier, NN)
    return jnp.where(used, place, -1.0)


def translate_and_pack(cells_ref, by_offset_ref, ids_ref, operator_ref, block, picked, terms, signed, store):
    coefs, cells = cells_ref.shape
    offsets, slots = by_offset_ref.shape
    peers = ids_ref.shape[0]
    sign = degree_signs(WIDE)
    block[coefs // 8 * 8 :, :] = jnp.zeros((WIDE - coefs // 8 * 8, cells), F32)
    block[:coefs, :] = cells_ref[...]
    held = turned_terms(block[...])
    for o in range(0, offsets, 2):
        chosen = jnp.concatenate(
            [source_indicator(by_offset_ref[i : i + 1, :], cells) for i in (o, o + 1)], axis=0
        )
        columns = halves(dot(chosen, held, NN))
        picked[o * slots : (o + 2) * slots, :] = columns * sign if signed else columns
    for o in range(offsets):
        moved = translate(picked[o * slots : (o + 1) * slots, :], operator_ref[o])
        terms[:, o] = (moved * sign if signed else moved).reshape(peers, -1, WIDE)
    place = positions(ids_ref[...])
    for p in range(peers):
        pick = target_indicator(place[p : p + 1, :], PACK)
        store(p, halves(dot(pick, both_terms(terms[p].reshape(-1, WIDE), 1), NN)))


def listed_kernel(cells_ref, by_offset_ref, ids_ref, operator_ref, out_ref, block, picked, terms):
    def store(p, value):
        out_ref[p] = value

    translate_and_pack(
        cells_ref, by_offset_ref, ids_ref, operator_ref, block, picked, terms, False, store
    )


def answer_kernel(
    cells_ref, by_offset_ref, ids_ref, operator_ref, listed_ref, out_ref, block, picked, terms
):
    def store(p, value):
        out_ref[p, :PACK] = listed_ref[p]
        out_ref[p, PACK:] = value

    translate_and_pack(
        cells_ref, by_offset_ref, ids_ref, operator_ref, block, picked, terms, True, store
    )


def pack_ids(ids):
    place = positions(ids)
    value = ids + 1.0
    high = jnp.floor(value * (1.0 / 32.0))
    low = value - 32.0 * high
    packed = []
    for p in range(ids.shape[0]):
        pick = target_indicator(place[p : p + 1, :], PACK)
        both = jnp.concatenate([high[p : p + 1], low[p : p + 1]], axis=0).astype(BF16)
        both = dot(both, pick, NT)
        packed.append(32.0 * both[:1] + both[1:] - 1.0)
    return jnp.concatenate(packed, axis=0)


def target_kernel(their_ref, own_ref, out_ref):
    out_ref[...] = jnp.concatenate([pack_ids(their_ref[...]), pack_ids(own_ref[...])], axis=1)


def message_kernel(target_ref, count_ref, top_ref, out_ref):
    peers, room, offsets = target_ref.shape
    coefs = top_ref.shape[1]
    counts = count_ref[...]
    for c in range(room):
        ids = jnp.where(c < counts, target_ref[:, c, :], -1).astype(F32)
        out_ref[:, 0, c * offsets : (c + 1) * offsets] = ids
    out_ref[:, 1, :coefs] = jnp.broadcast_to(top_ref[...], (peers, coefs))
    out_ref[:, 1, coefs:] = jnp.zeros((peers, WIDE - coefs), F32)


def sum_kernel(terms_ref, target_ref, near_ref, out_ref, total):
    coefs, cells = out_ref.shape
    peers = terms_ref.shape[0]
    total[...] = jnp.zeros_like(total)
    for p in range(0, peers, 2):
        terms = jnp.concatenate([terms_ref[p], terms_ref[p + 1]], axis=0)
        target = jnp.concatenate([target_ref[p : p + 1, :], target_ref[p + 1 : p + 2, :]], axis=1)
        total[...] += dot(target_indicator(target, cells), both_terms(terms, 1), NN)
    result = near_ref[...] + halves(total[...])
    out_ref[...] = jnp.transpose(result)[:coefs, :]


def grid(segs):
    ys = 1
    while ys * ys < segs:
        ys *= 2
    return segs // ys, ys


def body(
    multipoles,
    top_multipoles,
    translators,
    child_shifts,
    far_operator,
    far_weights,
    cell_codes,
    inner_sources,
    inner_targets,
    pair_sources,
    peer_target_cells,
    pair_counts,
):
    coefs, cells = multipoles.shape
    parents = far_weights.shape[0]
    peers, offsets, room = pair_sources.shape[1:]
    slots = offsets * room
    pad = WIDE - coefs
    segs = lax.axis_size("seg")
    params = pltpu.CompilerParams(vmem_limit_bytes=48 * 1024 * 1024)

    message = pl.pallas_call(
        message_kernel,
        out_shape=jax.ShapeDtypeStruct((peers, 2, WIDE), F32),
        name="message",
    )(peer_target_cells[0].transpose(0, 2, 1), pair_counts[0], top_multipoles.reshape(1, coefs))
    arrived = lax.all_to_all(message, "sub", split_axis=0, concat_axis=0, tiled=True)
    their_target, tops = arrived[:, 0].reshape(peers, room, offsets), arrived[:, 1]

    def by_peer(ids):
        return ids.transpose(0, 2, 1).reshape(peers, slots).astype(F32)

    def by_offset(ids):
        return ids.transpose(2, 0, 1).reshape(offsets, -1).astype(F32)

    used = lax.broadcasted_iota(jnp.int32, (peers, room, offsets), 1) < pair_counts[0][:, None, :]
    own_source = jnp.where(used, pair_sources[0].transpose(0, 2, 1), -1)
    operators = three_terms(translators)
    scratch = [
        pltpu.VMEM((WIDE, cells), F32),
        pltpu.VMEM((offsets * peers * room, WIDE), F32),
        pltpu.VMEM((peers, offsets, room, WIDE), F32),
    ]
    pair_cost = pl.CostEstimate(flops=2 * 10**9, bytes_accessed=3 * 10**6, transcendentals=0)
    listed = pl.pallas_call(
        listed_kernel,
        out_shape=jax.ShapeDtypeStruct((peers, PACK, WIDE), F32),
        scratch_shapes=scratch,
        compiler_params=params,
        cost_estimate=pair_cost,
        name="listed_terms",
    )(multipoles, by_offset(own_source), by_peer(own_source), operators)
    tops, listed = lax.optimization_barrier((tops, listed))

    xs, ys = grid(segs)
    core = lax.axis_index("sub") % 2
    half = peers // 2
    mine = lax.dynamic_slice_in_dim(tops, core * half, half, axis=0)
    spread = lax.all_to_all(
        jnp.broadcast_to(mine[None], (max(xs // 2, 1) * ys, half, WIDE)),
        "seg",
        split_axis=0,
        concat_axis=0,
        tiled=True,
        axis_index_groups=[[x * ys + y for x in range(odd, xs, 2) for y in range(ys)] for odd in range(min(xs, 2))],
    )


    packet = pl.pallas_call(
        answer_kernel,
        out_shape=jax.ShapeDtypeStruct((peers, 2 * PACK, WIDE), F32),
        scratch_shapes=scratch,
        compiler_params=params,
        cost_estimate=pair_cost,
        name="answers",
    )(multipoles, by_offset(their_target), by_peer(their_target), operators, listed)
    packet, spread = lax.optimization_barrier((packet, spread))
    received = lax.all_to_all(packet, "sub", split_axis=0, concat_axis=0, tiled=True)

    last, first = multipoles[:, cells - HALO :], multipoles[:, :HALO]
    block = spread.reshape(1, -1, WIDE)
    if xs > 1:
        pairs = [(x * ys + y, (x ^ 1) * ys + y) for x in range(xs) for y in range(ys)]
        block = jnp.concatenate([block, lax.ppermute(block, "seg", pairs)], axis=0)
    every_top = lax.all_gather(
        block,
        "sub",
        axis=0,
        tiled=True,
        axis_index_groups=[[2 * i, 2 * i + 1] for i in range(half)],
    )
    every_top = every_top.reshape(2, xs, ys, half, WIDE)
    place_x = (lax.axis_index("seg") // ys).astype(jnp.int32).reshape(1)
    up = [(i, i + 1) for i in range(segs - 1)]
    down = [(j, i) for i, j in up]
    before = lax.ppermute(last, "seg", up)
    after = lax.ppermute(first, "seg", down)
    window = jnp.concatenate([before, multipoles, after], axis=1)
    span = cells + WIDE
    window = jnp.pad(window, ((0, pad), (0, span - window.shape[1])))

    targets = pl.pallas_call(
        target_kernel,
        out_shape=jax.ShapeDtypeStruct((peers, 2 * PACK), F32),
        compiler_params=params,
        name="packed_targets",
    )(by_peer(their_target), by_peer(own_source))

    shifts = jnp.pad(child_shifts, ((0, 0), (0, pad), (0, pad)))
    far = jnp.pad(far_operator, ((0, pad), (0, pad)))

    inner_rows = inner_sources.shape[1] * inner_sources.shape[2] // 128
    near = pl.pallas_call(
        inner_kernel,
        out_shape=jax.ShapeDtypeStruct((cells, WIDE), F32),
        scratch_shapes=[
            pltpu.VMEM((inner_rows * 128, WIDE), F32),
            pltpu.VMEM((cells, 2 * WIDE), F32),
        ],
        compiler_params=params,
        cost_estimate=pl.CostEstimate(flops=2 * 10**9, bytes_accessed=3 * 10**6, transcendentals=0),
        name="inner_pairs",
    )(
        window,
        inner_sources[0].reshape(inner_rows, 128).astype(F32),
        inner_targets[0].reshape(inner_rows, 128).astype(F32),
        operators,
    )

    octants = child_shifts.shape[0]
    place = (cell_codes % octants * parents + cell_codes // octants).astype(F32)
    near = pl.pallas_call(
        far_kernel,
        in_specs=[pl.BlockSpec(memory_space=pltpu.SMEM)] + [pl.BlockSpec(memory_space=pltpu.VMEM)] * 6,
        out_shape=jax.ShapeDtypeStruct((cells, WIDE), F32),
        compiler_params=params,
        cost_estimate=pl.CostEstimate(flops=10**9, bytes_accessed=2 * 10**6, transcendentals=0),
        name="far_field",
    )(place_x, every_top, far_weights, far, shifts, place, near)

    return pl.pallas_call(
        sum_kernel,
        out_shape=jax.ShapeDtypeStruct((coefs, cells), F32),
        scratch_shapes=[pltpu.VMEM((cells, 2 * WIDE), F32)],
        compiler_params=params,
        cost_estimate=pl.CostEstimate(flops=2 * 10**9, bytes_accessed=3 * 10**6, transcendentals=0),
        name="sum_terms",
    )(received, targets, near)


def solution(mesh):
    in_specs = (
        P(None, ("seg", "sub")),
        P(None, ("seg", "sub")),
        P(),
        P(),
        P(),
        P(("seg", "sub"), None),
        P(("seg", "sub"), None),
        P(("seg", "sub"), None, None),
        P(("seg", "sub"), None, None),
        P(("seg", "sub"), None, None, None),
        P(("seg", "sub"), None, None, None),
        P(("seg", "sub"), None, None),
    )
    out_specs = P(None, ("seg", "sub"))
    return jax.shard_map(body, mesh=mesh, in_specs=in_specs, out_specs=out_specs, check_vma=False)
```
